32 devices in a mesh: expert: 16 (over z, y, x), fsdp: 2 (over core).
Axes of the slice: x: 2, y: 2, z: 4, core: 2. Of those that a mesh axis runs over, the one named last changes fastest.
Arguments:
- tokens: bfloat16 [4096, 768], P(('expert', 'fsdp')), may hold values from -12 to 12
- cotangent: bfloat16 [4096, 768], P(('expert', 'fsdp')), may hold values from -6 to 6
- qkv_weight: bfloat16 [768, 2304], P('fsdp'), may hold values from -0.21875 to 0.21875
- qkv_moment: float32 [32, 55296], P(('expert', 'fsdp')), may hold values from -40 to 40
- qkv_square: float32 [32, 55296], P(('expert', 'fsdp')), may hold values from 4.096 to 16.384
- out_weight: bfloat16 [768, 768], P('fsdp'), may hold values from -1.75 to 1.75
- out_moment: float32 [32, 18432], P(('expert', 'fsdp')), may hold values from -4 to 4
- out_square: float32 [32, 18432], P(('expert', 'fsdp')), may hold values from 0.04096 to 0.16384
- up_experts: bfloat16 [16, 768, 1536], P('expert', None, 'fsdp'), may hold values from -0.21875 to 0.21875
- up_moment: float32 [16, 768, 1536], P('expert', None, 'fsdp'), may hold values from -6 to 6
- up_square: float32 [16, 768, 1536], P('expert', None, 'fsdp'), may hold values from 0.08192 to 0.3328
- down_experts: bfloat16 [16, 1536, 768], P('expert', 'fsdp'), may hold values from -1.25 to 1.25
- down_moment: float32 [16, 1536, 768], P('expert', 'fsdp'), may hold values from -1.25 to 1.25
- down_square: float32 [16, 1536, 768], P('expert', 'fsdp'), may hold values from 0.0034 to 0.0136
- router_weight: bfloat16 [768, 8], replicated, may hold values from -0.109375 to 0.109375
- router_moment: float32 [768, 8], replicated, may hold values from -448 to 448
- router_square: float32 [768, 8], replicated, may hold values from 393.216 to 1572.864
- norm_gains: bfloat16 [2, 768], replicated, may hold values from 0.5 to 1.5
- gain_moment: float32 [2, 768], replicated, may hold values from -40 to 40
- gain_square: float32 [2, 768], replicated, may hold values from 4.096 to 16.384
- relative_position_bias: bfloat16 [32, 12], replicated, may hold values from -6 to 6
- bias_moment: float32 [32, 12], replicated, may hold values from -128 to 128
- bias_square: float32 [32, 12], replicated, may hold values from 41.94304 to 167.77216
- expert_ids: int32 [4096], P(('expert', 'fsdp')), may hold values from 0 to 7, as said below
- slot_ids: int32 [4096], P(('expert', 'fsdp')), may hold values from -1 to 19, as said below
Outputs:
- block_out: bfloat16 [4096, 768], P(('expert', 'fsdp'))
- tokens_grad: float32 [4096, 768], P(('expert', 'fsdp'))
- new_qkv_moment: float32 [32, 55296], P(('expert', 'fsdp'))
- new_qkv_square: float32 [32, 55296], P(('expert', 'fsdp'))
- new_qkv_weight: float32 [32, 55296], P(('expert', 'fsdp'))
- new_out_moment: float32 [32, 18432], P(('expert', 'fsdp'))
- new_out_square: float32 [32, 18432], P(('expert', 'fsdp'))
- new_out_weight: float32 [32, 18432], P(('expert', 'fsdp'))
- new_up_moment: float32 [16, 768, 1536], P('expert', None, 'fsdp')
- new_up_square: float32 [16, 768, 1536], P('expert', None, 'fsdp')
- new_up_experts: float32 [16, 768, 1536], P('expert', None, 'fsdp')
- new_down_moment: float32 [16, 1536, 768], P('expert', 'fsdp')
- new_down_square: float32 [16, 1536, 768], P('expert', 'fsdp')
- new_down_experts: float32 [16, 1536, 768], P('expert', 'fsdp')
- new_router_moment: float32 [768, 8], replicated
- new_router_square: float32 [768, 8], replicated
- new_router_weight: float32 [768, 8], replicated
- new_gain_moment: float32 [2, 768], replicated
- new_gain_square: float32 [2, 768], replicated
- new_gains: float32 [2, 768], replicated
- new_bias_moment: float32 [32, 12], replicated
- new_bias_square: float32 [32, 12], replicated
- new_rel_bias: float32 [32, 12], replicated
The draws below stay inside these ranges and needn't reach their ends.
Inputs may be any that keep to these rules, and one draw needn't show every extreme that they name: `expert_ids`: every expert is chosen by some token of the first device. `slot_ids`: for each token, the number of earlier tokens of the same device with the same expert, or -1 where that number is 20 or more. On every device some expert fills all 20 slots.
All inputs are finite; a program needn't handle non-finite values.
Results may differ from the reference program's by a relative error of at most 0.014.
Values may be sent and summed in bfloat16 or wider, within the bound.
A program may use at most 128 MiB of HBM per device.

```python
import math
import jax
import jax.numpy as jnp
from jax import lax

D = 768
HEADS = 12
FF = 3072
BUCKETS = 32
STEP = 10
TOK_DEV = 128
EXPERTS = 8
CAP = 20
SEQ = 256
SHARDS = 32
TOKENS = 4096
QBLK = 55296
OBLK = 18432
N_EXPERT = 16
N_FSDP = 2


def route_table(key):
    block_count = TOKENS // TOK_DEV
    sub_keys = jax.random.split(key, 6)
    first_pick = jax.random.randint(sub_keys[0], (block_count, TOK_DEV), 0, EXPERTS)
    second_pick = jax.random.randint(sub_keys[1], (block_count, TOK_DEV), 0, EXPERTS)
    third_pick = jax.random.randint(sub_keys[2], (block_count, TOK_DEV), 0, EXPERTS)
    ranked = jnp.minimum(jnp.minimum(first_pick, second_pick), third_pick)
    expert_order = jax.random.permutation(sub_keys[3], EXPERTS).astype(jnp.int32)
    chosen = expert_order[ranked]
    hot_expert = jax.random.randint(sub_keys[4], (), 0, EXPERTS)
    noise_bits = jax.random.randint(sub_keys[5], (block_count, TOK_DEV), 0, 2 ** 20)
    unique_score = noise_bits * TOK_DEV + jnp.arange(TOK_DEV, dtype=jnp.int32)[None, :]
    rank_pos = jnp.argsort(jnp.argsort(unique_score, axis=1), axis=1).astype(jnp.int32)
    chosen = jnp.where(rank_pos < CAP, hot_expert, chosen)
    cover_rank = rank_pos - CAP
    cover_mask = (cover_rank >= 0) & (cover_rank < EXPERTS) & (jnp.arange(block_count, dtype=jnp.int32)[:, None] == 0)
    chosen = jnp.where(cover_mask, expert_order[jnp.clip(cover_rank, 0, EXPERTS - 1)], chosen)
    indicator_matrix = (chosen[:, :, None] == jnp.arange(EXPERTS, dtype=jnp.int32)[None, None, :]).astype(jnp.int32)
    before = jnp.cumsum(indicator_matrix, axis=1) - indicator_matrix
    earlier = jnp.sum(before * indicator_matrix, axis=2)
    slot_table = jnp.where(earlier < CAP, earlier, -1)
    return (chosen.reshape(TOKENS).astype(jnp.int32), slot_table.reshape(TOKENS).astype(jnp.int32))


def draw_expert_ids(key, part):
    shared = route_table(key)
    return shared[0]


def draw_slot_ids(key, part):
    shared = route_table(key)
    return shared[1]


def strengthened(values, stream_key, source, target, blocks, factor):
    owner, partner = [(jnp.arange(values.shape[axis_at]) // (values.shape[axis_at] // blocks)).reshape([-1 if axis == axis_at else 1 for axis in range(values.ndim)]) for axis_at in (source, target)]
    chosen = jax.random.permutation(stream_key, blocks)[partner]
    strong = (owner == chosen) | (owner == (partner + blocks // 2) % blocks)
    return jnp.where(strong, factor * values, values)


def level_of(stream_key, extent, pieces, low, top_value):
    level, own = 1.0, jax.random.fold_in(stream_key, 6)
    for dim, blocks in pieces:
        heights = jnp.exp(jax.random.uniform(jax.random.fold_in(own, dim), (blocks,), jnp.float32, low / len(pieces), top_value / len(pieces)))
        level = level * jnp.repeat(heights, extent[dim] // blocks).reshape([-1 if axis == dim else 1 for axis in range(len(extent))])
    return level


def centred(stream_key, extent, scale, reach, shards=(), kind=jnp.bfloat16):
    entries = jax.random.normal(stream_key, extent, jnp.float32) * scale
    if len(shards) > 0:
        entries = level_of(stream_key, extent, shards, -0.22, 0.18) * entries
    return jnp.clip(entries, min=-reach, max=reach).astype(kind)


def noise_with(key, extent, spread, most, cuts, heavy, held_as=jnp.bfloat16):
    values = spread * jax.random.normal(key, extent, jnp.float32)
    if cuts:
        values = values * level_of(key, extent, cuts, -0.22, 0.18)
    return jnp.clip(strengthened(values, jax.random.fold_in(key, 3), *heavy), -most, most).astype(held_as)


def setup_inputs(seed: int = 0) -> dict:
    keys = jax.random.split(jax.random.key(seed), 26)
    return {
        "tokens": noise_with(keys[0], (TOKENS, D), 1.0, 12.0, ((0, 32),), (0, 1, 32, 2.75)),
        "cotangent": centred(keys[1], (TOKENS, D), 1.0, 6.0, ((0, 32),)),
        "qkv_weight": centred(keys[2], (D, 3 * D), D ** -0.5, 0.21875, ((0, 2),)),
        "qkv_moment": centred(keys[3], (SHARDS, QBLK), (0.11 * TOKENS ** 0.5), 40.0, ((0, 32),), jnp.float32),
        "qkv_square": jnp.clip(jnp.exp(math.log(16.384) - 1.3862944 * jax.random.uniform(keys[4], (SHARDS, QBLK), jnp.float32) ** level_of(keys[4], (SHARDS, QBLK), ((0, 32),), -0.2, 0.2)), 4.096, 16.384),
        "out_weight": centred(keys[5], (D, D), ((SEQ // 4) ** 0.5 * D ** -0.5), 1.75, ((0, 2),)),
        "out_moment": centred(keys[6], (SHARDS, OBLK), (0.011 * TOKENS ** 0.5), 4.0, ((0, 32),), jnp.float32),
        "out_square": jnp.clip(jnp.exp(math.log(0.16384) - 1.3862944 * jax.random.uniform(keys[7], (SHARDS, OBLK), jnp.float32) ** level_of(keys[7], (SHARDS, OBLK), ((0, 32),), -0.2, 0.2)), 0.04096, 0.16384),
        "up_experts": centred(keys[8], (N_EXPERT, D, FF // 2), D ** -0.5, 0.21875, ((0, 16), (2, 2))),
        "up_moment": centred(keys[9], (N_EXPERT, D, FF // 2), (0.062 * SEQ ** 0.5), 6.0, ((0, 16), (2, 2)), jnp.float32),
        "up_square": jnp.clip(jnp.exp(math.log(0.3328) - 1.4017986 * jax.random.uniform(keys[10], (N_EXPERT, D, FF // 2), jnp.float32) ** level_of(keys[10], (N_EXPERT, D, FF // 2), ((0, 16), (2, 2)), -0.2, 0.2)), 0.08192, 0.3328),
        "down_experts": centred(keys[11], (N_EXPERT, FF // 2, D), (1.5 * EXPERTS * FF ** -0.5), 1.25, ((0, 16), (1, 2))),
        "down_moment": centred(keys[12], (N_EXPERT, FF // 2, D), (0.1 * SEQ ** 0.5 * EXPERTS ** -1), 1.25, ((0, 16), (1, 2)), jnp.float32),
        "down_square": jnp.clip(jnp.exp(math.log(0.0136) - 1.3862944 * jax.random.uniform(keys[13], (N_EXPERT, FF // 2, D), jnp.float32) ** level_of(keys[13], (N_EXPERT, FF // 2, D), ((0, 16), (1, 2)), -0.2, 0.2)), 0.0034, 0.0136),
        "router_weight": centred(keys[14], (D, EXPERTS), (4 * D) ** -0.5, 0.109375),
        "router_moment": centred(keys[15], (D, EXPERTS), (0.16 * (D * SEQ) ** 0.5), 448.0, (), jnp.float32),
        "router_square": jnp.clip(jnp.exp(jax.random.uniform(keys[16], (D, EXPERTS), jnp.float32, math.log(393.216), math.log(1572.864))), 393.216, 1572.864),
        "norm_gains": jnp.clip(1.0 + 0.1 * jax.random.normal(keys[17], (2, D), jnp.float32), 0.5, 1.5).astype(jnp.bfloat16),
        "gain_moment": centred(keys[18], (2, D), (0.11 * TOKENS ** 0.5), 40.0, (), jnp.float32),
        "gain_square": jnp.clip(jnp.exp(jax.random.uniform(keys[19], (2, D), jnp.float32, math.log(4.096), math.log(16.384))), 4.096, 16.384),
        "relative_position_bias": centred(keys[20], (BUCKETS, HEADS), 1.0, 6.0),
        "bias_moment": centred(keys[21], (BUCKETS, HEADS), (0.022 * (TOKENS * SEQ) ** 0.5), 128.0, (), jnp.float32),
        "bias_square": jnp.clip(jnp.exp(jax.random.uniform(keys[22], (BUCKETS, HEADS), jnp.float32, math.log(41.94304), math.log(167.77216))), 41.94304, 167.77216),
        "expert_ids": draw_expert_ids(jax.random.fold_in(keys[25], 71), 0),
        "slot_ids": draw_slot_ids(jax.random.fold_in(keys[25], 71), 0),
    }


@jax.custom_vjp
def low(v):
    return lax.optimization_barrier(v.astype(jnp.bfloat16)).astype(jnp.float32)

@jax.custom_vjp
def low_back(v):
    return v

def low_keep(v):
    return (low(v), None)

def low_pass(kept, grad):
    return (grad,)

def back_keep(v):
    return (v, None)

def back_low(kept, grad):
    return (low(grad),)
low.defvjp(low_keep, low_pass)
low_back.defvjp(back_keep, back_low)
EPS_NORM = 1e-06
BETA_ONE = 0.9
BETA_TWO = 0.999
ADAM_EPS = 1e-08
DECAY = 0.1

def exact_dot(left, right):
    return jnp.dot(left, right, precision=lax.Precision.HIGHEST)

def rms_norm(value, gain):
    return value * lax.rsqrt(lax.optimization_barrier(jnp.mean(value * value, axis=-1, keepdims=True)) + EPS_NORM) * gain

def bucket_ids(query_pos, key_pos):
    relative = key_pos[None, :] - query_pos[:, None]
    distance = jnp.abs(relative)
    far_bucket = jnp.full(distance.shape, 8, jnp.int32)
    for degree in range(1, 8):
        far_bucket = far_bucket + (distance * distance >= 2 ** (degree + 6)).astype(jnp.int32)
    return jnp.where(distance < 8, distance, far_bucket) + 16 * (relative > 0).astype(jnp.int32)

def forward(inputs, qkv_weight, out_weight, up_experts, down_experts, router_weight, norm_gains, relative_position_bias, expert_ids, slot_ids):
    head_size = D // HEADS
    score_scale = head_size ** (-0.5)
    normed = low(rms_norm(inputs, norm_gains[0]))
    qkv = low_back(low(exact_dot(normed, qkv_weight)))
    positions = jnp.arange(SEQ, dtype=jnp.int32)
    bias_table = jnp.transpose(relative_position_bias[bucket_ids(positions, positions)], (2, 0, 1))

    def attend(seq_rows):
        queries = seq_rows[:, :D].reshape(SEQ, HEADS, head_size)
        keys_all = seq_rows[:, D:2 * D].reshape(SEQ, HEADS, head_size)
        values_all = seq_rows[:, 2 * D:].reshape(SEQ, HEADS, head_size)
        scores = jnp.einsum('qhd,khd->hqk', queries, keys_all, precision=lax.Precision.HIGHEST) * score_scale + bias_table
        scores = low_back(scores)
        log_total = jax.nn.logsumexp(scores, axis=-1, keepdims=True)
        prob_low = low(jnp.exp(scores - log_total))
        return jnp.einsum('hqk,khd->qhd', prob_low, values_all, precision=lax.Precision.HIGHEST).reshape(SEQ, D)
    context = lax.map(jax.checkpoint(attend), qkv.reshape(TOKENS // SEQ, SEQ, 3 * D)).reshape(TOKENS, D)
    context = low_back(low(context))
    attention = low_back(exact_dot(context, out_weight))
    middle = inputs + attention
    normed_two = rms_norm(middle, norm_gains[1])
    router_probs = jax.nn.softmax(exact_dot(normed_two, router_weight), axis=-1)
    gate_prob = jnp.take_along_axis(router_probs, expert_ids[:, None], axis=1)[:, 0]
    partition_count = N_EXPERT * N_FSDP
    device_of = jnp.arange(TOKENS, dtype=jnp.int32) // TOK_DEV
    is_kept = slot_ids >= 0
    slot_place = jnp.where(is_kept, expert_ids * CAP + slot_ids, EXPERTS * CAP)
    buffer_rows = jnp.zeros((partition_count, EXPERTS * CAP + 1, D), jnp.float32).at[device_of, slot_place].set(low(normed_two))
    dispatched = buffer_rows[:, :EXPERTS * CAP].reshape(partition_count, EXPERTS, CAP, D)
    dispatched = jnp.transpose(dispatched, (1, 0, 2, 3)).reshape(EXPERTS, partition_count * CAP, D)
    up_full = jnp.transpose(up_experts.reshape(EXPERTS, 2, D, FF // 2), (0, 2, 1, 3)).reshape(EXPERTS, D, FF)
    down_full = down_experts.reshape(EXPERTS, FF, D)

    def expert_ffn(expert_args):
        rows_here, up_here, down_here = expert_args
        pre_act = low_back(exact_dot(rows_here, up_here))
        activation_output = low(jax.nn.gelu(pre_act, approximate=False))
        return exact_dot(activation_output, down_here)
    expert_rows = lax.map(jax.checkpoint(expert_ffn), (dispatched, up_full, down_full))
    expert_rows = low_back(expert_rows)
    expert_rows = jnp.transpose(expert_rows.reshape(EXPERTS, partition_count, CAP, D), (1, 0, 2, 3)).reshape(partition_count, EXPERTS * CAP, D)
    picked = expert_rows[device_of, jnp.where(is_kept, slot_place, 0)]
    expert_mix = jnp.where(is_kept[:, None], gate_prob[:, None] * picked, 0.0)
    return middle + expert_mix

def adam_step(weight, moment, square, grad, rate, decay):
    new_moment = BETA_ONE * moment + (1.0 - BETA_ONE) * grad
    new_square = BETA_TWO * square + (1.0 - BETA_TWO) * grad * grad
    moment_hat = new_moment / (1.0 - BETA_ONE ** STEP)
    square_hat = new_square / (1.0 - BETA_TWO ** STEP)
    new_weight = weight - rate * (moment_hat / (jnp.sqrt(square_hat) + ADAM_EPS) + decay * weight)
    return (new_moment, new_square, new_weight)

def reference(tokens, cotangent, qkv_weight, qkv_moment, qkv_square, out_weight, out_moment, out_square, up_experts, up_moment, up_square, down_experts, down_moment, down_square, router_weight, router_moment, router_square, norm_gains, gain_moment, gain_square, relative_position_bias, bias_moment, bias_square, expert_ids, slot_ids):
    qkv_float = qkv_weight.astype(jnp.float32)
    out_float = out_weight.astype(jnp.float32)
    up_float = up_experts.astype(jnp.float32)
    down_float = down_experts.astype(jnp.float32)
    router_float = router_weight.astype(jnp.float32)
    gain_float = norm_gains.astype(jnp.float32)
    bias_float = relative_position_bias.astype(jnp.float32)

    def layer(inputs, qkv_w, out_w, up_w, down_w, router_w, gain_w, bias_w):
        return forward(inputs, qkv_w, out_w, up_w, down_w, router_w, gain_w, bias_w, expert_ids, slot_ids)
    result, pullback = jax.vjp(layer, tokens.astype(jnp.float32), qkv_float, out_float, up_float, down_float, router_float, gain_float, bias_float)
    all_grads = pullback(cotangent.astype(jnp.float32))
    partition_count = N_EXPERT * N_FSDP
    qkv_m, qkv_v, qkv_w = adam_step(qkv_float.reshape(partition_count, -1), qkv_moment, qkv_square, all_grads[1].reshape(partition_count, -1), 2.0 * D ** (-0.5), DECAY)
    out_m, out_v, out_w = adam_step(out_float.reshape(partition_count, -1), out_moment, out_square, all_grads[2].reshape(partition_count, -1), (SEQ / D) ** 0.5, DECAY)
    up_m, up_v, up_w = adam_step(up_float, up_moment, up_square, all_grads[3], 2.0 * D ** (-0.5), DECAY)
    down_m, down_v, down_w = adam_step(down_float, down_moment, down_square, all_grads[4], 3.0 * EXPERTS * FF ** (-0.5), DECAY)
    router_m, router_v, router_w = adam_step(router_float, router_moment, router_square, all_grads[5], D ** (-0.5), DECAY)
    gain_m, gain_v, gain_w = adam_step(gain_float, gain_moment, gain_square, all_grads[6], 0.5, 0.0)
    bias_m, bias_v, bias_w = adam_step(bias_float, bias_moment, bias_square, all_grads[7], 2.0, 0.0)
    return (result.astype(jnp.bfloat16), all_grads[0], qkv_m, qkv_v, qkv_w, out_m, out_v, out_w, up_m, up_v, up_w, down_m, down_v, down_w, router_m, router_v, router_w, gain_m, gain_v, gain_w, bias_m, bias_v, bias_w)
```

```python
import jax
import jax.numpy as jnp
from jax import lax
from jax.sharding import PartitionSpec as P

FF = 3072
STEP = 10


EPS_NORM = 1e-06
BETA_ONE = 0.9
BETA_TWO = 0.999
ADAM_EPS = 1e-08
DECAY = 0.1
ROOT_HALF = 0.7071067811865476
INV_ROOT_TWO_PI = 0.3989422804014327


def norm_forward(value, gain):
    inverse = lax.rsqrt(jnp.mean(value * value, axis=-1, keepdims=True) + EPS_NORM)
    return (value * inverse * gain, inverse)


def norm_backward(value, inverse, gain, upstream):
    scaled = upstream * gain
    normal = value * inverse
    gain_grad = jnp.sum(normal * upstream, axis=0)
    value_grad = inverse * (scaled - normal * jnp.mean(normal * scaled, axis=-1, keepdims=True))
    return (value_grad, gain_grad)


def gelu_value(value):
    return 0.5 * value * (1.0 + lax.erf(value * ROOT_HALF))


def gelu_derivative(value):
    return (
        0.5 * (1.0 + lax.erf(value * ROOT_HALF))
        + value * jnp.exp(-0.5 * value * value) * INV_ROOT_TWO_PI
    )


def bucket_ids(query_pos, key_pos):
    relative = key_pos[None, :] - query_pos[:, None]
    distance = jnp.abs(relative)
    far_bucket = jnp.full(distance.shape, 8, jnp.int32)
    for degree in range(1, 8):
        far_bucket = far_bucket + (distance * distance >= 2 ** (degree + 6)).astype(jnp.int32)
    return jnp.where(distance < 8, distance, far_bucket) + 16 * (relative > 0).astype(jnp.int32)


def adam_step(weight, moment, square, grad, rate, decay):
    new_moment = BETA_ONE * moment + (1.0 - BETA_ONE) * grad
    new_square = BETA_TWO * square + (1.0 - BETA_TWO) * grad * grad
    moment_hat = new_moment / (1.0 - BETA_ONE**STEP)
    square_hat = new_square / (1.0 - BETA_TWO**STEP)
    new_weight = weight - rate * (moment_hat / (jnp.sqrt(square_hat) + ADAM_EPS) + decay * weight)
    return (new_moment, new_square, new_weight)


def swap(value):
    return lax.ppermute(value, "fsdp", ((0, 1), (1, 0)))


def bit_swap(value, bit):
    size = lax.axis_size("expert")
    return lax.ppermute(value, "expert", tuple((i, i ^ (1 << bit)) for i in range(size)))


def sum_to_owner(grad, order):
    n_expert = lax.axis_size("expert")
    bits = n_expert.bit_length() - 1
    rows, columns = grad.shape
    block = rows // (2 * n_expert)
    core = lax.axis_index("fsdp")
    place = lax.axis_index("expert")
    pieces = grad.reshape((n_expert, 2, block, columns))
    kept = lax.dynamic_index_in_dim(pieces, core, 1, keepdims=False)
    sent = lax.dynamic_index_in_dim(pieces, 1 - core, 1, keepdims=False)
    total = kept + swap(sent.astype(jnp.bfloat16)).astype(jnp.float32)
    total = total.reshape((2,) * bits + (block, columns))
    left = list(range(bits - 1, -1, -1))
    for bit in order:
        axis = left.index(bit)
        left.remove(bit)
        mine = (place >> bit) & 1
        sent = lax.dynamic_index_in_dim(total, 1 - mine, axis, keepdims=False)
        kept = lax.dynamic_index_in_dim(total, mine, axis, keepdims=False)
        total = kept + bit_swap(sent.astype(jnp.bfloat16), bit).astype(jnp.float32)
    return total


def sum_everywhere(value):
    bits = lax.axis_size("expert").bit_length() - 1
    value = value + swap(value)
    for bit in range(bits):
        value = value + bit_swap(value, bit)
    return value


def local(
    tokens,
    cotangent,
    qkv_weight,
    qkv_moment,
    qkv_square,
    out_weight,
    out_moment,
    out_square,
    up_experts,
    up_moment,
    up_square,
    down_experts,
    down_moment,
    down_square,
    router_weight,
    router_moment,
    router_square,
    norm_gains,
    gain_moment,
    gain_square,
    relative_position_bias,
    bias_moment,
    bias_square,
    expert_ids,
    slot_ids,
):
    tok_rows, model_width = tokens.shape
    bucket_count, head_count = relative_position_bias.shape
    head_size = model_width // head_count
    score_scale = head_size ** (-0.5)
    expert_count = router_weight.shape[1]
    n_expert = lax.axis_size("expert")
    n_fsdp = lax.axis_size("fsdp")
    bits = n_expert.bit_length() - 1
    capacity = 2 * (5 * tok_rows // (4 * n_expert))
    seq_len = tok_rows * n_fsdp
    half = model_width // 2
    core = lax.axis_index("fsdp")
    own_index = lax.axis_index("expert") * n_fsdp + core
    qkv_other = swap(qkv_weight)
    out_other = swap(out_weight)
    inputs = tokens.astype(jnp.float32)
    upstream = cotangent.astype(jnp.float32)
    gain_one = norm_gains[0].astype(jnp.float32)
    gain_two = norm_gains[1].astype(jnp.float32)
    normed, inverse_one = norm_forward(inputs, gain_one)
    normed_low = normed.astype(jnp.bfloat16)

    def own_part(value):
        return lax.dynamic_slice_in_dim(value, core * half, half, 1)

    def other_part(value):
        return lax.dynamic_slice_in_dim(value, (1 - core) * half, half, 1)

    def times_halves(value, own, other):
        return jnp.dot(own_part(value), own, preferred_element_type=jnp.float32) + jnp.dot(
            other_part(value), other, preferred_element_type=jnp.float32
        )

    def times_transposed(value, own, other):
        first = jnp.where(core == 0, own, other)
        second = jnp.where(core == 0, other, own)
        return jnp.concatenate(
            [
                jnp.einsum("te,de->td", value, first, preferred_element_type=jnp.float32),
                jnp.einsum("te,de->td", value, second, preferred_element_type=jnp.float32),
            ],
            axis=1,
        )

    query_pos = core * tok_rows + jnp.arange(tok_rows, dtype=jnp.int32)
    other_pos = (1 - core) * tok_rows + jnp.arange(tok_rows, dtype=jnp.int32)
    key_pos = jnp.concatenate([query_pos, other_pos])
    bucket_range = jnp.arange(bucket_count, dtype=jnp.int32)
    indicator = (bucket_ids(query_pos, key_pos)[None] == bucket_range[:, None, None]).astype(
        jnp.bfloat16
    )
    bias_block = jnp.einsum(
        "yur,yv->vur", indicator, relative_position_bias, preferred_element_type=jnp.float32
    )
    qkv = times_halves(normed_low, qkv_weight, qkv_other).astype(jnp.bfloat16)
    key_value = qkv[:, model_width:]
    both = jnp.concatenate([key_value, swap(key_value)], axis=0)
    keys_heads = both[:, :model_width].reshape(seq_len, head_count, head_size)
    values_heads = both[:, model_width:].reshape(seq_len, head_count, head_size)
    queries = qkv[:, :model_width].reshape(tok_rows, head_count, head_size)
    scores = (
        jnp.einsum("qhd,khd->hqk", queries, keys_heads, preferred_element_type=jnp.float32)
        * score_scale
        + bias_block
    )
    log_total = jax.nn.logsumexp(scores, axis=-1, keepdims=True)
    prob_full = jnp.exp(scores - log_total)
    prob_low = prob_full.astype(jnp.bfloat16)
    context = (
        jnp.einsum("hqk,khd->qhd", prob_low, values_heads, preferred_element_type=jnp.float32)
        .astype(jnp.bfloat16)
        .reshape(tok_rows, model_width)
    )
    attention = times_halves(context, out_weight, out_other)
    middle = inputs + attention
    normed_two, inverse_two = norm_forward(middle, gain_two)
    router_float = router_weight.astype(jnp.float32)
    logits = jnp.dot(normed_two, router_float, precision=lax.Precision.HIGHEST)
    router_probs = jax.nn.softmax(logits, axis=-1)
    is_chosen = expert_ids[:, None] == jnp.arange(expert_count, dtype=jnp.int32)[None, :]
    gate_prob = jnp.sum(jnp.where(is_chosen, router_probs, 0.0), axis=1)
    slot_rows = n_expert * capacity
    row_range = jnp.arange(slot_rows, dtype=jnp.int32)
    row_expert = row_range // (2 * capacity)
    row_slot = row_range % capacity
    pick = (
        (row_expert[None, :] == expert_ids[:, None]) & (row_slot[None, :] == slot_ids[:, None])
    ).astype(jnp.bfloat16)
    token_rows = jnp.concatenate(
        [normed_two.astype(jnp.bfloat16), (gate_prob[:, None] * upstream).astype(jnp.bfloat16)],
        axis=1,
    )
    dispatched = jnp.einsum(
        "tr,td->rd", pick, token_rows, preferred_element_type=jnp.float32
    ).astype(jnp.bfloat16)
    arrived = lax.all_to_all(
        dispatched.reshape(n_expert, capacity, 2 * model_width),
        "expert",
        split_axis=0,
        concat_axis=0,
        tiled=True,
    ).reshape(slot_rows, 2 * model_width)
    up_local = up_experts[0]
    down_local = down_experts[0]
    gathered = jnp.concatenate([arrived, swap(arrived)], axis=0)
    expert_in = gathered[:, :model_width]
    grad_in = gathered[:, model_width:]
    pre_act = jnp.dot(expert_in, up_local, preferred_element_type=jnp.float32)
    activated = gelu_value(pre_act).astype(jnp.bfloat16)
    act_grad = jnp.einsum("rd,hd->rh", grad_in, down_local, preferred_element_type=jnp.float32)
    pre_grad = (act_grad * gelu_derivative(pre_act)).astype(jnp.bfloat16)
    partial_rows = jnp.concatenate(
        [
            jnp.dot(activated, down_local, preferred_element_type=jnp.float32),
            jnp.einsum("rh,dh->rd", pre_grad, up_local, preferred_element_type=jnp.float32),
        ],
        axis=1,
    )
    from_other = swap(partial_rows[slot_rows:].astype(jnp.bfloat16))
    summed = (partial_rows[:slot_rows] + from_other.astype(jnp.float32)).astype(jnp.bfloat16)
    returned = lax.all_to_all(
        summed.reshape(n_expert, capacity, 2 * model_width),
        "expert",
        split_axis=0,
        concat_axis=0,
        tiled=True,
    ).reshape(slot_rows, 2 * model_width)
    up_grad = jnp.einsum("rd,rh->dh", expert_in, pre_grad, preferred_element_type=jnp.float32)
    down_grad = jnp.einsum("rh,rd->hd", activated, grad_in, preferred_element_type=jnp.float32)
    mixed = jnp.dot(pick, returned, preferred_element_type=jnp.float32)
    picked = mixed[:, :model_width]
    dispatch_grad = mixed[:, model_width:]
    block_out = (middle + gate_prob[:, None] * picked).astype(jnp.bfloat16)
    gate_grad = jnp.sum(upstream * picked, axis=1)
    logit_grad = (gate_grad * gate_prob)[:, None] * (is_chosen.astype(jnp.float32) - router_probs)
    router_grad = jnp.dot(logit_grad.T, normed_two, precision=lax.Precision.HIGHEST)
    normed_two_grad = dispatch_grad + jnp.dot(
        logit_grad, router_float.T, precision=lax.Precision.HIGHEST
    )
    middle_part, gain_two_grad = norm_backward(middle, inverse_two, gain_two, normed_two_grad)
    middle_grad = upstream + middle_part
    attention_grad = middle_grad.astype(jnp.bfloat16)
    out_weight_grad = jnp.einsum(
        "td,te->de", context, attention_grad, preferred_element_type=jnp.float32
    )
    context_grad = (
        times_transposed(attention_grad, out_weight, out_other)
        .astype(jnp.bfloat16)
        .reshape(tok_rows, head_count, head_size)
    )
    prob_grad = jnp.einsum(
        "qhd,khd->hqk", context_grad, values_heads, preferred_element_type=jnp.float32
    )
    score_grad = (
        prob_full * (prob_grad - jnp.sum(prob_full * prob_grad, axis=-1, keepdims=True))
    ).astype(jnp.bfloat16)
    value_grad = jnp.einsum(
        "hqk,qhd->khd", prob_low, context_grad, preferred_element_type=jnp.float32
    ).reshape(seq_len, model_width)
    key_grad = (
        jnp.einsum("hqk,qhd->khd", score_grad, queries, preferred_element_type=jnp.float32)
        * score_scale
    ).reshape(seq_len, model_width)
    key_value_grad = jnp.concatenate([key_grad, value_grad], axis=1)
    key_value_own = (
        key_value_grad[:tok_rows]
        + swap(key_value_grad[tok_rows:].astype(jnp.bfloat16)).astype(jnp.float32)
    ).astype(jnp.bfloat16)
    query_grad = (
        (
            jnp.einsum("hqk,khd->qhd", score_grad, keys_heads, preferred_element_type=jnp.float32)
            * score_scale
        )
        .astype(jnp.bfloat16)
        .reshape(tok_rows, model_width)
    )
    table_grad = jnp.einsum(
        "evf,uvf->eu", indicator, score_grad, preferred_element_type=jnp.float32
    )
    qkv_grad = jnp.concatenate([query_grad, key_value_own], axis=1)

    def weight_grad(upstream_part):
        return jnp.einsum(
            "td,te->de", normed_low, upstream_part, preferred_element_type=jnp.float32
        )

    upward = list(range(bits))
    out_sum = sum_to_owner(out_weight_grad, upward[2:] + upward[:2])
    query_sum = sum_to_owner(weight_grad(query_grad), upward)
    key_sum = sum_to_owner(
        weight_grad(key_value_own[:, :model_width]), upward[1:] + upward[:1]
    )
    value_sum = sum_to_owner(
        weight_grad(key_value_own[:, model_width:]), upward[2:] + upward[:2]
    )
    normed_grad = times_transposed(qkv_grad, qkv_weight, qkv_other)
    input_part, gain_one_grad = norm_backward(inputs, inverse_one, gain_one, normed_grad)
    tokens_grad = middle_grad + input_part
    table_size = bucket_count * head_count
    small = jnp.concatenate(
        [
            router_grad,
            gain_one_grad[None],
            gain_two_grad[None],
            jnp.pad(table_grad.reshape(1, table_size), ((0, 0), (0, model_width - table_size))),
        ],
        axis=0,
    )
    small = sum_everywhere(small)
    router_sum = small[:expert_count].T
    gain_sum = small[expert_count : expert_count + 2]
    table_sum = small[expert_count + 2, :table_size].reshape(bucket_count, head_count)
    qkv_sum = jnp.concatenate([query_sum, key_sum, value_sum], axis=1).reshape(1, -1)
    block = model_width // (n_expert * n_fsdp)
    first_row = own_index * block
    owner_core = first_row // half
    local_row = first_row - owner_core * half

    def old_rows(own, other):
        own_rows = lax.dynamic_slice_in_dim(own, local_row, block, 0)
        other_rows = lax.dynamic_slice_in_dim(other, local_row, block, 0)
        rows = jnp.where(owner_core == core, own_rows, other_rows)
        return rows.astype(jnp.float32).reshape(1, -1)

    qkv_old = old_rows(qkv_weight, qkv_other)
    out_old = old_rows(out_weight, out_other)
    out_sum = out_sum.reshape(1, -1)
    qkv_m, qkv_v, qkv_w = adam_step(
        qkv_old, qkv_moment, qkv_square, qkv_sum, 2.0 * model_width ** (-0.5), DECAY
    )
    out_m, out_v, out_w = adam_step(
        out_old, out_moment, out_square, out_sum, (seq_len / model_width) ** 0.5, DECAY
    )
    up_m, up_v, up_w = adam_step(
        up_experts.astype(jnp.float32),
        up_moment,
        up_square,
        up_grad[None],
        2.0 * model_width ** (-0.5),
        DECAY,
    )
    down_m, down_v, down_w = adam_step(
        down_experts.astype(jnp.float32),
        down_moment,
        down_square,
        down_grad[None],
        3.0 * expert_count * FF ** (-0.5),
        DECAY,
    )
    router_m, router_v, router_w = adam_step(
        router_float, router_moment, router_square, router_sum, model_width ** (-0.5), DECAY
    )
    gain_m, gain_v, gain_w = adam_step(
        norm_gains.astype(jnp.float32), gain_moment, gain_square, gain_sum, 0.5, 0.0
    )
    bias_m, bias_v, bias_w = adam_step(
        relative_position_bias.astype(jnp.float32), bias_moment, bias_square, table_sum, 2.0, 0.0
    )
    return (
        block_out,
        tokens_grad,
        qkv_m,
        qkv_v,
        qkv_w,
        out_m,
        out_v,
        out_w,
        up_m,
        up_v,
        up_w,
        down_m,
        down_v,
        down_w,
        router_m,
        router_v,
        router_w,
        gain_m,
        gain_v,
        gain_w,
        bias_m,
        bias_v,
        bias_w,
    )


def solution(mesh):
    return jax.shard_map(
        local,
        mesh=mesh,
        in_specs=(
            P(("expert", "fsdp"), None),
            P(("expert", "fsdp"), None),
            P("fsdp", None),
            P(("expert", "fsdp"), None),
            P(("expert", "fsdp"), None),
            P("fsdp", None),
            P(("expert", "fsdp"), None),
            P(("expert", "fsdp"), None),
            P("expert", None, "fsdp"),
            P("expert", None, "fsdp"),
            P("expert", None, "fsdp"),
            P("expert", "fsdp", None),
            P("expert", "fsdp", None),
            P("expert", "fsdp", None),
            P(),
            P(),
            P(),
            P(),
            P(),
            P(),
            P(),
            P(),
            P(),
            P(("expert", "fsdp")),
            P(("expert", "fsdp")),
        ),
        out_specs=(
            P(("expert", "fsdp"), None),
            P(("expert", "fsdp"), None),
            P(("expert", "fsdp"), None),
            P(("expert", "fsdp"), None),
            P(("expert", "fsdp"), None),
            P(("expert", "fsdp"), None),
            P(("expert", "fsdp"), None),
            P(("expert", "fsdp"), None),
            P("expert", None, "fsdp"),
            P("expert", None, "fsdp"),
            P("expert", None, "fsdp"),
            P("expert", "fsdp", None),
            P("expert", "fsdp", None),
            P("expert", "fsdp", None),
            P(),
            P(),
            P(),
            P(),
            P(),
            P(),
            P(),
            P(),
            P(),
        ),
        check_vma=False,
    )
```

```python
import functools
import itertools

import jax
import jax.numpy as jnp
from jax import lax
from jax.experimental import pallas as pl
from jax.experimental.pallas import tpu as pltpu
from jax.sharding import PartitionSpec as P

FF = 3072
STEP = 10


EPS_NORM = 1e-06
BETA_ONE = 0.9
BETA_TWO = 0.999
ADAM_EPS = 1e-08
DECAY = 0.1
ROOT_HALF = 0.7071067811865476
INV_ROOT_TWO_PI = 0.3989422804014327


def norm_forward(value, gain):
    inverse = lax.rsqrt(jnp.mean(value * value, axis=-1, keepdims=True) + EPS_NORM)
    return (value * inverse * gain, inverse)


def norm_backward(value, inverse, gain, upstream):
    scaled = upstream * gain
    normal = value * inverse
    gain_grad = jnp.sum(normal * upstream, axis=0)
    value_grad = inverse * (scaled - normal * jnp.mean(normal * scaled, axis=-1, keepdims=True))
    return (value_grad, gain_grad)


def gelu_value(value):
    return 0.5 * value * (1.0 + lax.erf(value * ROOT_HALF))


def gelu_derivative(value):
    return (
        0.5 * (1.0 + lax.erf(value * ROOT_HALF))
        + value * jnp.exp(-0.5 * value * value) * INV_ROOT_TWO_PI
    )


def bucket_ids(query_pos, key_pos):
    relative = key_pos[None, :] - query_pos[:, None]
    distance = jnp.abs(relative)
    far_bucket = jnp.full(distance.shape, 8, jnp.int32)
    for degree in range(1, 8):
        far_bucket = far_bucket + (distance * distance >= 2 ** (degree + 6)).astype(jnp.int32)
    return jnp.where(distance < 8, distance, far_bucket) + 16 * (relative > 0).astype(jnp.int32)


def adam_step(weight, moment, square, grad, rate, decay):
    new_moment = BETA_ONE * moment + (1.0 - BETA_ONE) * grad
    new_square = BETA_TWO * square + (1.0 - BETA_TWO) * grad * grad
    moment_hat = new_moment / (1.0 - BETA_ONE**STEP)
    square_hat = new_square / (1.0 - BETA_TWO**STEP)
    new_weight = weight - rate * (moment_hat / (jnp.sqrt(square_hat) + ADAM_EPS) + decay * weight)
    return (new_moment, new_square, new_weight)


def swap(value):
    return lax.ppermute(value, "fsdp", ((0, 1), (1, 0)))


def bit_swap(value, bit):
    size = lax.axis_size("expert")
    return lax.ppermute(value, "expert", tuple((i, i ^ (1 << bit)) for i in range(size)))


def sum_to_owner(grad, order):
    n_expert = lax.axis_size("expert")
    bits = n_expert.bit_length() - 1
    rows, columns = grad.shape
    block = rows // (2 * n_expert)
    core = lax.axis_index("fsdp")
    place = lax.axis_index("expert")
    pieces = grad.reshape((n_expert, 2, block, columns))
    kept = lax.dynamic_index_in_dim(pieces, core, 1, keepdims=False)
    sent = lax.dynamic_index_in_dim(pieces, 1 - core, 1, keepdims=False)
    total = kept + swap(sent.astype(jnp.bfloat16)).astype(jnp.float32)
    total = total.reshape((2,) * bits + (block, columns))
    left = list(range(bits - 1, -1, -1))
    for bit in order:
        axis = left.index(bit)
        left.remove(bit)
        mine = (place >> bit) & 1
        sent = lax.dynamic_index_in_dim(total, 1 - mine, axis, keepdims=False)
        kept = lax.dynamic_index_in_dim(total, mine, axis, keepdims=False)
        total = kept + bit_swap(sent.astype(jnp.bfloat16), bit).astype(jnp.float32)
    return total


def sum_everywhere(value):
    bits = lax.axis_size("expert").bit_length() - 1
    value = value + swap(value)
    for bit in range(bits):
        value = value + bit_swap(value, bit)
    return value


def owner_sum_kernel(bits, orders, grad, small, total, small_total, held, *rest):
    landed, (small_held, small_landed, send_sem, recv_sem, small_send, small_recv) = (
        rest[: bits + 1],
        rest[bits + 1 :],
    )
    pieces = len(orders)
    core = lax.axis_index("fsdp")
    place = lax.axis_index("expert")
    mine = [lax.rem(lax.div(place, 1 << bit), 2) for bit in range(bits)]
    partners = [{"fsdp": 1 - core}] + [
        {"expert": place + (1 - 2 * mine[bit]) * (1 << bit)} for bit in range(bits)
    ]

    def mesh_copy(source, target, sent, received, partner):
        return pltpu.make_async_remote_copy(
            src_ref=source,
            dst_ref=target,
            send_sem=sent,
            recv_sem=received,
            device_id=partner,
            device_id_type=pl.DeviceIdType.MESH,
        )

    barrier = pltpu.get_barrier_semaphore()
    for partner in partners:
        pl.semaphore_signal(
            barrier, inc=1, device_id=partner, device_id_type=pl.DeviceIdType.MESH
        )
    pl.semaphore_wait(barrier, len(partners))

    def piece_copy(piece, step):
        sent, received = send_sem.at[piece, step], recv_sem.at[piece, step]
        if step == 0:
            return mesh_copy(
                grad.at[1 - core, piece], landed[0].at[piece], sent, received, partners[0]
            )
        order = orders[piece]
        place_of = [slice(None)] * bits
        for bit in order[: step - 1]:
            place_of[bits - 1 - bit] = mine[bit]
        bit = order[step - 1]
        place_of[bits - 1 - bit] = 1 - mine[bit]
        return mesh_copy(
            held.at[(piece, *place_of)],
            landed[step].at[piece],
            sent,
            received,
            partners[1 + bit],
        )

    def small_copy(step):
        bit = step - 1
        return mesh_copy(
            small if step == 0 else small_held.at[step - 1],
            small_landed.at[step],
            small_send.at[step],
            small_recv.at[step],
            partners[1 + bit],
        )

    def add_part(piece, step, side):
        order = orders[piece]
        fixed = order[:step]
        split = order[step] if step < bits else None
        open_bits = [bit for bit in range(bits - 1, -1, -1) if bit not in fixed]
        free_bits = [bit for bit in open_bits if bit != split]
        for combo in itertools.product((0, 1), repeat=len(free_bits)):
            values = dict(zip(free_bits, combo))
            if split is not None:
                values[split] = mine[split] if side else 1 - mine[split]
            arrived_at = tuple(values[bit] for bit in open_bits)
            for bit in fixed:
                values[bit] = mine[bit]
            held_at = tuple(values[bit] for bit in range(bits - 1, -1, -1))
            arrived = landed[step][(piece, *arrived_at)].astype(jnp.float32)
            if step == 0:
                before = grad[(core, piece, *held_at)].astype(jnp.float32)
            else:
                before = held[(piece, *held_at)].astype(jnp.float32)
            if split is None:
                total[piece] = before + arrived
            else:
                held[(piece, *held_at)] = (before + arrived).astype(held.dtype)

    for piece in range(pieces):
        piece_copy(piece, 0).start()
    small_copy(0).start()
    for step in range(bits + 1):
        for piece in range(pieces):
            piece_copy(piece, step).wait_recv()
            if step < bits:
                add_part(piece, step, 0)
                piece_copy(piece, step + 1).start()
            add_part(piece, step, 1)
        small_copy(step).wait_recv()
        before = small[...] if step == 0 else small_held[step - 1]
        if step < bits:
            small_held[step] = before + small_landed[step]
            small_copy(step + 1).start()
        else:
            small_total[...] = before + small_landed[step]
    for step in range(bits + 1):
        for piece in range(pieces):
            piece_copy(piece, step).wait_send()
        small_copy(step).wait_send()


def owner_sum(grad, small):
    n_expert = lax.axis_size("expert")
    bits = n_expert.bit_length() - 1
    rows, columns = grad.shape
    block = rows // (2 * n_expert)
    pieces = 3
    width = columns // (2 * pieces)
    order = list(range(bits))
    orders = [order[shift:] + order[:shift] for shift in range(pieces)]
    spread = (
        grad.astype(jnp.bfloat16)
        .reshape(n_expert, 2, block, pieces, 2, width)
        .transpose(1, 3, 0, 4, 2, 5)
        .reshape((2, pieces) + (2,) * bits + (2 * block, width))
    )
    vmem = pl.BlockSpec(memory_space=pltpu.VMEM)
    slots = [
        pltpu.VMEM((pieces,) + (2,) * (bits - step) + (2 * block, width), jnp.bfloat16)
        for step in [0] + list(range(bits + 1))
    ]
    total, small_total = pl.pallas_call(
        functools.partial(owner_sum_kernel, bits, orders),
        out_shape=(
            jax.ShapeDtypeStruct((pieces, 2 * block, width), jnp.float32),
            jax.ShapeDtypeStruct(small.shape, jnp.float32),
        ),
        in_specs=[vmem, vmem],
        out_specs=(vmem, vmem),
        scratch_shapes=slots
        + [
            pltpu.VMEM((bits,) + small.shape, jnp.float32),
            pltpu.VMEM((bits + 1,) + small.shape, jnp.float32),
            pltpu.SemaphoreType.DMA((pieces, bits + 1)),
            pltpu.SemaphoreType.DMA((pieces, bits + 1)),
            pltpu.SemaphoreType.DMA((bits + 1,)),
            pltpu.SemaphoreType.DMA((bits + 1,)),
        ],
        compiler_params=pltpu.CompilerParams(
            collective_id=0, has_side_effects=True, vmem_limit_bytes=32 * 2**20
        ),
    )(spread, small)
    total = total.reshape(pieces, 2, block, width).transpose(2, 0, 1, 3).reshape(block, columns)
    return total, small_total


def local(
    tokens,
    cotangent,
    qkv_weight,
    qkv_moment,
    qkv_square,
    out_weight,
    out_moment,
    out_square,
    up_experts,
    up_moment,
    up_square,
    down_experts,
    down_moment,
    down_square,
    router_weight,
    router_moment,
    router_square,
    norm_gains,
    gain_moment,
    gain_square,
    relative_position_bias,
    bias_moment,
    bias_square,
    expert_ids,
    slot_ids,
):
    tok_rows, model_width = tokens.shape
    bucket_count, head_count = relative_position_bias.shape
    head_size = model_width // head_count
    score_scale = head_size ** (-0.5)
    expert_count = router_weight.shape[1]
    n_expert = lax.axis_size("expert")
    n_fsdp = lax.axis_size("fsdp")
    bits = n_expert.bit_length() - 1
    capacity = 2 * (5 * tok_rows // (4 * n_expert))
    seq_len = tok_rows * n_fsdp
    half = model_width // 2
    core = lax.axis_index("fsdp")
    own_index = lax.axis_index("expert") * n_fsdp + core
    qkv_other = swap(qkv_weight)
    out_other = swap(out_weight)
    inputs = tokens.astype(jnp.float32)
    upstream = cotangent.astype(jnp.float32)
    gain_one = norm_gains[0].astype(jnp.float32)
    gain_two = norm_gains[1].astype(jnp.float32)
    normed, inverse_one = norm_forward(inputs, gain_one)
    normed_low = normed.astype(jnp.bfloat16)

    def own_part(value):
        return lax.dynamic_slice_in_dim(value, core * half, half, 1)

    def other_part(value):
        return lax.dynamic_slice_in_dim(value, (1 - core) * half, half, 1)

    def times_halves(value, own, other):
        return jnp.dot(own_part(value), own, preferred_element_type=jnp.float32) + jnp.dot(
            other_part(value), other, preferred_element_type=jnp.float32
        )

    def times_transposed(value, own, other):
        first = jnp.where(core == 0, own, other)
        second = jnp.where(core == 0, other, own)
        return jnp.concatenate(
            [
                jnp.einsum("te,de->td", value, first, preferred_element_type=jnp.float32),
                jnp.einsum("te,de->td", value, second, preferred_element_type=jnp.float32),
            ],
            axis=1,
        )

    query_pos = core * tok_rows + jnp.arange(tok_rows, dtype=jnp.int32)
    other_pos = (1 - core) * tok_rows + jnp.arange(tok_rows, dtype=jnp.int32)
    key_pos = jnp.concatenate([query_pos, other_pos])
    bucket_range = jnp.arange(bucket_count, dtype=jnp.int32)
    indicator = (bucket_ids(query_pos, key_pos)[None] == bucket_range[:, None, None]).astype(
        jnp.bfloat16
    )
    bias_block = jnp.einsum(
        "yur,yv->vur", indicator, relative_position_bias, preferred_element_type=jnp.float32
    )
    qkv = times_halves(normed_low, qkv_weight, qkv_other).astype(jnp.bfloat16)
    key_value = qkv[:, model_width:]
    both = jnp.concatenate([key_value, swap(key_value)], axis=0)
    keys_heads = both[:, :model_width].reshape(seq_len, head_count, head_size)
    values_heads = both[:, model_width:].reshape(seq_len, head_count, head_size)
    queries = qkv[:, :model_width].reshape(tok_rows, head_count, head_size)
    scores = (
        jnp.einsum("qhd,khd->hqk", queries, keys_heads, preferred_element_type=jnp.float32)
        * score_scale
        + bias_block
    )
    log_total = jax.nn.logsumexp(scores, axis=-1, keepdims=True)
    prob_full = jnp.exp(scores - log_total)
    prob_low = prob_full.astype(jnp.bfloat16)
    context = (
        jnp.einsum("hqk,khd->qhd", prob_low, values_heads, preferred_element_type=jnp.float32)
        .astype(jnp.bfloat16)
        .reshape(tok_rows, model_width)
    )
    attention = times_halves(context, out_weight, out_other)
    middle = inputs + attention
    normed_two, inverse_two = norm_forward(middle, gain_two)
    router_float = router_weight.astype(jnp.float32)
    logits = jnp.dot(normed_two, router_float, precision=lax.Precision.HIGHEST)
    router_probs = jax.nn.softmax(logits, axis=-1)
    is_chosen = expert_ids[:, None] == jnp.arange(expert_count, dtype=jnp.int32)[None, :]
    gate_prob = jnp.sum(jnp.where(is_chosen, router_probs, 0.0), axis=1)
    slot_rows = n_expert * capacity
    row_range = jnp.arange(slot_rows, dtype=jnp.int32)
    row_expert = row_range // (2 * capacity)
    row_slot = row_range % capacity
    pick = (
        (row_expert[None, :] == expert_ids[:, None]) & (row_slot[None, :] == slot_ids[:, None])
    ).astype(jnp.bfloat16)
    token_rows = jnp.concatenate(
        [normed_two.astype(jnp.bfloat16), (gate_prob[:, None] * upstream).astype(jnp.bfloat16)],
        axis=1,
    )
    dispatched = jnp.einsum(
        "tr,td->rd", pick, token_rows, preferred_element_type=jnp.float32
    ).astype(jnp.bfloat16)
    arrived = lax.all_to_all(
        dispatched.reshape(n_expert, capacity, 2 * model_width),
        "expert",
        split_axis=0,
        concat_axis=0,
        tiled=True,
    ).reshape(slot_rows, 2 * model_width)
    up_local = up_experts[0]
    down_local = down_experts[0]
    gathered = jnp.concatenate([arrived, swap(arrived)], axis=0)
    expert_in = gathered[:, :model_width]
    grad_in = gathered[:, model_width:]
    pre_act = jnp.dot(expert_in, up_local, preferred_element_type=jnp.float32)
    activated = gelu_value(pre_act).astype(jnp.bfloat16)
    act_grad = jnp.einsum("rd,hd->rh", grad_in, down_local, preferred_element_type=jnp.float32)
    pre_grad = (act_grad * gelu_derivative(pre_act)).astype(jnp.bfloat16)
    partial_rows = jnp.concatenate(
        [
            jnp.dot(activated, down_local, preferred_element_type=jnp.float32),
            jnp.einsum("rh,dh->rd", pre_grad, up_local, preferred_element_type=jnp.float32),
        ],
        axis=1,
    )
    from_other = swap(partial_rows[slot_rows:].astype(jnp.bfloat16))
    summed = (partial_rows[:slot_rows] + from_other.astype(jnp.float32)).astype(jnp.bfloat16)
    returned = lax.all_to_all(
        summed.reshape(n_expert, capacity, 2 * model_width),
        "expert",
        split_axis=0,
        concat_axis=0,
        tiled=True,
    ).reshape(slot_rows, 2 * model_width)
    up_grad = jnp.einsum("rd,rh->dh", expert_in, pre_grad, preferred_element_type=jnp.float32)
    down_grad = jnp.einsum("rh,rd->hd", activated, grad_in, preferred_element_type=jnp.float32)
    mixed = jnp.dot(pick, returned, preferred_element_type=jnp.float32)
    picked = mixed[:, :model_width]
    dispatch_grad = mixed[:, model_width:]
    block_out = (middle + gate_prob[:, None] * picked).astype(jnp.bfloat16)
    gate_grad = jnp.sum(upstream * picked, axis=1)
    logit_grad = (gate_grad * gate_prob)[:, None] * (is_chosen.astype(jnp.float32) - router_probs)
    router_grad = jnp.dot(logit_grad.T, normed_two, precision=lax.Precision.HIGHEST)
    normed_two_grad = dispatch_grad + jnp.dot(
        logit_grad, router_float.T, precision=lax.Precision.HIGHEST
    )
    middle_part, gain_two_grad = norm_backward(middle, inverse_two, gain_two, normed_two_grad)
    middle_grad = upstream + middle_part
    attention_grad = middle_grad.astype(jnp.bfloat16)
    out_weight_grad = jnp.einsum(
        "td,te->de", context, attention_grad, preferred_element_type=jnp.float32
    )
    context_grad = (
        times_transposed(attention_grad, out_weight, out_other)
        .astype(jnp.bfloat16)
        .reshape(tok_rows, head_count, head_size)
    )
    prob_grad = jnp.einsum(
        "qhd,khd->hqk", context_grad, values_heads, preferred_element_type=jnp.float32
    )
    score_grad = (
        prob_full * (prob_grad - jnp.sum(prob_full * prob_grad, axis=-1, keepdims=True))
    ).astype(jnp.bfloat16)
    value_grad = jnp.einsum(
        "hqk,qhd->khd", prob_low, context_grad, preferred_element_type=jnp.float32
    ).reshape(seq_len, model_width)
    key_grad = (
        jnp.einsum("hqk,qhd->khd", score_grad, queries, preferred_element_type=jnp.float32)
        * score_scale
    ).reshape(seq_len, model_width)
    key_value_grad = jnp.concatenate([key_grad, value_grad], axis=1)
    key_value_own = (
        key_value_grad[:tok_rows]
        + swap(key_value_grad[tok_rows:].astype(jnp.bfloat16)).astype(jnp.float32)
    ).astype(jnp.bfloat16)
    query_grad = (
        (
            jnp.einsum("hqk,khd->qhd", score_grad, keys_heads, preferred_element_type=jnp.float32)
            * score_scale
        )
        .astype(jnp.bfloat16)
        .reshape(tok_rows, model_width)
    )
    table_grad = jnp.einsum(
        "evf,uvf->eu", indicator, score_grad, preferred_element_type=jnp.float32
    )
    qkv_grad = jnp.concatenate([query_grad, key_value_own], axis=1)

    def weight_grad(upstream_part):
        return jnp.einsum(
            "td,te->de", normed_low, upstream_part, preferred_element_type=jnp.float32
        )

    normed_grad = times_transposed(qkv_grad, qkv_weight, qkv_other)
    input_part, gain_one_grad = norm_backward(inputs, inverse_one, gain_one, normed_grad)
    tokens_grad = middle_grad + input_part
    table_size = bucket_count * head_count
    small = jnp.concatenate(
        [
            router_grad,
            gain_one_grad[None],
            gain_two_grad[None],
            jnp.pad(table_grad.reshape(1, table_size), ((0, 0), (0, model_width - table_size))),
        ],
        axis=0,
    )
    block = model_width // (n_expert * n_fsdp)
    if block % 8 == 0:
        small = jnp.pad(small, ((0, -small.shape[0] % 8), (0, 0)))
        weight_sum, small = owner_sum(
            jnp.concatenate([weight_grad(qkv_grad), out_weight_grad], axis=1), small
        )
        qkv_sum = weight_sum[:, : 3 * model_width].reshape(1, -1)
        out_sum = weight_sum[:, 3 * model_width :].reshape(1, -1)
    else:
        upward = list(range(bits))
        small = sum_everywhere(small)
        qkv_sum = sum_to_owner(weight_grad(qkv_grad), upward).reshape(1, -1)
        out_sum = sum_to_owner(out_weight_grad, upward[1:] + upward[:1]).reshape(1, -1)
    router_sum = small[:expert_count].T
    gain_sum = small[expert_count : expert_count + 2]
    table_sum = small[expert_count + 2, :table_size].reshape(bucket_count, head_count)
    first_row = own_index * block
    owner_core = first_row // half
    local_row = first_row - owner_core * half

    def old_rows(own, other):
        own_rows = lax.dynamic_slice_in_dim(own, local_row, block, 0)
        other_rows = lax.dynamic_slice_in_dim(other, local_row, block, 0)
        rows = jnp.where(owner_core == core, own_rows, other_rows)
        return rows.astype(jnp.float32).reshape(1, -1)

    qkv_old = old_rows(qkv_weight, qkv_other)
    out_old = old_rows(out_weight, out_other)
    qkv_m, qkv_v, qkv_w = adam_step(
        qkv_old, qkv_moment, qkv_square, qkv_sum, 2.0 * model_width ** (-0.5), DECAY
    )
    out_m, out_v, out_w = adam_step(
        out_old, out_moment, out_square, out_sum, (seq_len / model_width) ** 0.5, DECAY
    )
    up_m, up_v, up_w = adam_step(
        up_experts.astype(jnp.float32),
        up_moment,
        up_square,
        up_grad[None],
        2.0 * model_width ** (-0.5),
        DECAY,
    )
    down_m, down_v, down_w = adam_step(
        down_experts.astype(jnp.float32),
        down_moment,
        down_square,
        down_grad[None],
        3.0 * expert_count * FF ** (-0.5),
        DECAY,
    )
    router_m, router_v, router_w = adam_step(
        router_float, router_moment, router_square, router_sum, model_width ** (-0.5), DECAY
    )
    gain_m, gain_v, gain_w = adam_step(
        norm_gains.astype(jnp.float32), gain_moment, gain_square, gain_sum, 0.5, 0.0
    )
    bias_m, bias_v, bias_w = adam_step(
        relative_position_bias.astype(jnp.float32), bias_moment, bias_square, table_sum, 2.0, 0.0
    )
    return (
        block_out,
        tokens_grad,
        qkv_m,
        qkv_v,
        qkv_w,
        out_m,
        out_v,
        out_w,
        up_m,
        up_v,
        up_w,
        down_m,
        down_v,
        down_w,
        router_m,
        router_v,
        router_w,
        gain_m,
        gain_v,
        gain_w,
        bias_m,
        bias_v,
        bias_w,
    )


def solution(mesh):
    return jax.shard_map(
        local,
        mesh=mesh,
        in_specs=(
            P(("expert", "fsdp"), None),
            P(("expert", "fsdp"), None),
            P("fsdp", None),
            P(("expert", "fsdp"), None),
            P(("expert", "fsdp"), None),
            P("fsdp", None),
            P(("expert", "fsdp"), None),
            P(("expert", "fsdp"), None),
            P("expert", None, "fsdp"),
            P("expert", None, "fsdp"),
            P("expert", None, "fsdp"),
            P("expert", "fsdp", None),
            P("expert", "fsdp", None),
            P("expert", "fsdp", None),
            P(),
            P(),
            P(),
            P(),
            P(),
            P(),
            P(),
            P(),
            P(),
            P(("expert", "fsdp")),
            P(("expert", "fsdp")),
        ),
        out_specs=(
            P(("expert", "fsdp"), None),
            P(("expert", "fsdp"), None),
            P(("expert", "fsdp"), None),
            P(("expert", "fsdp"), None),
            P(("expert", "fsdp"), None),
            P(("expert", "fsdp"), None),
            P(("expert", "fsdp"), None),
            P(("expert", "fsdp"), None),
            P("expert", None, "fsdp"),
            P("expert", None, "fsdp"),
            P("expert", None, "fsdp"),
            P("expert", "fsdp", None),
            P("expert", "fsdp", None),
            P("expert", "fsdp", None),
            P(),
            P(),
            P(),
            P(),
            P(),
            P(),
            P(),
            P(),
            P(),
        ),
        check_vma=False,
    )
```

```python
import itertools

import jax
import jax.numpy as jnp
from jax import lax
from jax.experimental import pallas as pl
from jax.experimental.pallas import tpu as pltpu
from jax.sharding import PartitionSpec as P

FF = 3072
STEP = 10


EPS_NORM = 1e-06
BETA_ONE = 0.9
BETA_TWO = 0.999
ADAM_EPS = 1e-08
DECAY = 0.1
ROOT_HALF = 0.7071067811865476
INV_ROOT_TWO_PI = 0.3989422804014327


def norm_forward(value, gain):
    inverse = lax.rsqrt(jnp.mean(value * value, axis=-1, keepdims=True) + EPS_NORM)
    return (value * inverse * gain, inverse)


def norm_backward(value, inverse, gain, upstream):
    scaled = upstream * gain
    normal = value * inverse
    gain_grad = jnp.sum(normal * upstream, axis=0)
    value_grad = inverse * (scaled - normal * jnp.mean(normal * scaled, axis=-1, keepdims=True))
    return (value_grad, gain_grad)


def gelu_value(value):
    return 0.5 * value * (1.0 + lax.erf(value * ROOT_HALF))


def gelu_derivative(value):
    return (
        0.5 * (1.0 + lax.erf(value * ROOT_HALF))
        + value * jnp.exp(-0.5 * value * value) * INV_ROOT_TWO_PI
    )


def bucket_ids(query_pos, key_pos):
    relative = key_pos[None, :] - query_pos[:, None]
    distance = jnp.abs(relative)
    far_bucket = jnp.full(distance.shape, 8, jnp.int32)
    for degree in range(1, 8):
        far_bucket = far_bucket + (distance * distance >= 2 ** (degree + 6)).astype(jnp.int32)
    return jnp.where(distance < 8, distance, far_bucket) + 16 * (relative > 0).astype(jnp.int32)


def adam_step(weight, moment, square, grad, rate, decay):
    new_moment = BETA_ONE * moment + (1.0 - BETA_ONE) * grad
    new_square = BETA_TWO * square + (1.0 - BETA_TWO) * grad * grad
    moment_hat = new_moment / (1.0 - BETA_ONE**STEP)
    square_hat = new_square / (1.0 - BETA_TWO**STEP)
    new_weight = weight - rate * (moment_hat / (jnp.sqrt(square_hat) + ADAM_EPS) + decay * weight)
    return (new_moment, new_square, new_weight)


def swap(value):
    return lax.ppermute(value, "fsdp", ((0, 1), (1, 0)))


def bit_swap(value, bit):
    size = lax.axis_size("expert")
    return lax.ppermute(value, "expert", tuple((i, i ^ (1 << bit)) for i in range(size)))


def sum_to_owner(grad, order):
    n_expert = lax.axis_size("expert")
    bits = n_expert.bit_length() - 1
    rows, columns = grad.shape
    block = rows // (2 * n_expert)
    core = lax.axis_index("fsdp")
    place = lax.axis_index("expert")
    pieces = grad.reshape((n_expert, 2, block, columns))
    kept = lax.dynamic_index_in_dim(pieces, core, 1, keepdims=False)
    sent = lax.dynamic_index_in_dim(pieces, 1 - core, 1, keepdims=False)
    total = kept + swap(sent.astype(jnp.bfloat16)).astype(jnp.float32)
    total = total.reshape((2,) * bits + (block, columns))
    left = list(range(bits - 1, -1, -1))
    for bit in order:
        axis = left.index(bit)
        left.remove(bit)
        mine = (place >> bit) & 1
        sent = lax.dynamic_index_in_dim(total, 1 - mine, axis, keepdims=False)
        kept = lax.dynamic_index_in_dim(total, mine, axis, keepdims=False)
        total = kept + bit_swap(sent.astype(jnp.bfloat16), bit).astype(jnp.float32)
    return total


def sum_everywhere(value):
    bits = lax.axis_size("expert").bit_length() - 1
    value = value + swap(value)
    for bit in range(bits):
        value = value + bit_swap(value, bit)
    return value


def owner_sum_kernel(bits, orders, lefts, rights, small, total, small_total, grad, held, *rest):
    left_count = len(lefts)
    landed, (small_held, small_landed, send_sem, recv_sem, small_send, small_recv) = (
        rest[: bits + 1],
        rest[bits + 1 :],
    )
    pieces = len(orders)
    core = lax.axis_index("fsdp")
    place = lax.axis_index("expert")
    mine = [lax.rem(lax.div(place, 1 << bit), 2) for bit in range(bits)]
    partners = [{"fsdp": 1 - core}] + [
        {"expert": place + (1 - 2 * mine[bit]) * (1 << bit)} for bit in range(bits)
    ]

    def mesh_copy(source, target, sent, received, partner):
        return pltpu.make_async_remote_copy(
            src_ref=source,
            dst_ref=target,
            send_sem=sent,
            recv_sem=received,
            device_id=partner,
            device_id_type=pl.DeviceIdType.MESH,
        )

    barrier = pltpu.get_barrier_semaphore()
    for partner in partners:
        pl.semaphore_signal(
            barrier, inc=1, device_id=partner, device_id_type=pl.DeviceIdType.MESH
        )
    pl.semaphore_wait(barrier, len(partners))

    def piece_copy(piece, step):
        sent, received = send_sem.at[piece, step], recv_sem.at[piece, step]
        if step == 0:
            return mesh_copy(
                grad.at[1 - core, piece], landed[0].at[piece], sent, received, partners[0]
            )
        order = orders[piece]
        place_of = [slice(None)] * bits
        for bit in order[: step - 1]:
            place_of[bits - 1 - bit] = mine[bit]
        bit = order[step - 1]
        place_of[bits - 1 - bit] = 1 - mine[bit]
        return mesh_copy(
            held.at[(piece, *place_of)],
            landed[step].at[piece],
            sent,
            received,
            partners[1 + bit],
        )

    def small_copy(step):
        bit = step - 1
        return mesh_copy(
            small if step == 0 else small_held.at[step - 1],
            small_landed.at[step],
            small_send.at[step],
            small_recv.at[step],
            partners[1 + bit],
        )

    def add_part(piece, step, side):
        order = orders[piece]
        fixed = order[:step]
        split = order[step] if step < bits else None
        open_bits = [bit for bit in range(bits - 1, -1, -1) if bit not in fixed]
        free_bits = [bit for bit in open_bits if bit != split]
        for combo in itertools.product((0, 1), repeat=len(free_bits)):
            values = dict(zip(free_bits, combo))
            if split is not None:
                values[split] = mine[split] if side else 1 - mine[split]
            arrived_at = tuple(values[bit] for bit in open_bits)
            for bit in fixed:
                values[bit] = mine[bit]
            held_at = tuple(values[bit] for bit in range(bits - 1, -1, -1))
            arrived = landed[step][(piece, *arrived_at)].astype(jnp.float32)
            if step == 0:
                before = grad[(core, piece, *held_at)].astype(jnp.float32)
            else:
                before = held[(piece, *held_at)].astype(jnp.float32)
            if split is None:
                total[piece] = before + arrived
            else:
                held[(piece, *held_at)] = (before + arrived).astype(held.dtype)

    edges = [0]
    for right in rights:
        edges.append(edges[-1] + right.shape[1])
    width = grad.shape[-1]
    block = grad.shape[-2] // 2
    chunk = min(4, 1 << bits)

    def product(first_row, row_count, first_column):
        parts = []
        for index in range(left_count):
            begin = max(first_column, edges[index])
            end = min(first_column + width, edges[index + 1])
            if begin < end:
                parts.append(
                    jnp.dot(
                        lefts[index][first_row : first_row + row_count, :],
                        rights[index][:, begin - edges[index] : end - edges[index]],
                        preferred_element_type=jnp.float32,
                    )
                )
        return parts[0] if len(parts) == 1 else jnp.concatenate(parts, axis=1)

    def make_piece(piece):
        for first in range(0, 1 << bits, chunk):
            sides = [
                product(
                    first * 2 * block, chunk * 2 * block, (2 * piece + side) * width
                )
                for side in range(2)
            ]
            for offset in range(chunk):
                chip = first + offset
                chip_at = tuple((chip >> bit) & 1 for bit in range(bits - 1, -1, -1))
                for to_core in range(2):
                    row = (2 * offset + to_core) * block
                    joined = jnp.concatenate(
                        [side[row : row + block] for side in sides], axis=0
                    )
                    grad[(to_core, piece, *chip_at)] = joined.astype(grad.dtype)

    small_copy(0).start()
    for piece in range(pieces):
        make_piece(piece)
        piece_copy(piece, 0).start()
    for step in range(bits + 1):
        for piece in range(pieces):
            piece_copy(piece, step).wait_recv()
            if step < bits:
                add_part(piece, step, 0)
                piece_copy(piece, step + 1).start()
            add_part(piece, step, 1)
        small_copy(step).wait_recv()
        before = small[...] if step == 0 else small_held[step - 1]
        if step < bits:
            small_held[step] = before + small_landed[step]
            small_copy(step + 1).start()
        else:
            small_total[...] = before + small_landed[step]
    for step in range(bits + 1):
        for piece in range(pieces):
            piece_copy(piece, step).wait_send()
        small_copy(step).wait_send()


def owner_sum(lefts, rights, small):
    n_expert = lax.axis_size("expert")
    bits = n_expert.bit_length() - 1
    rows = lefts[0].shape[0]
    columns = sum(right.shape[1] for right in rights)
    block = rows // (2 * n_expert)
    pieces = 3
    width = columns // (2 * pieces)
    order = list(range(bits))
    orders = [order[shift:] + order[:shift] for shift in range(pieces)]
    vmem = pl.BlockSpec(memory_space=pltpu.VMEM)
    count = len(lefts)

    def kernel(*refs):
        owner_sum_kernel(bits, orders, refs[:count], refs[count : 2 * count], *refs[2 * count :])

    slots = [
        pltpu.VMEM((2, pieces) + (2,) * bits + (2 * block, width), jnp.bfloat16)
    ] + [
        pltpu.VMEM((pieces,) + (2,) * (bits - step) + (2 * block, width), jnp.bfloat16)
        for step in [0] + list(range(bits + 1))
    ]
    total, small_total = pl.pallas_call(
        kernel,
        out_shape=(
            jax.ShapeDtypeStruct((pieces, 2 * block, width), jnp.float32),
            jax.ShapeDtypeStruct(small.shape, jnp.float32),
        ),
        in_specs=[vmem] * (2 * count + 1),
        out_specs=(vmem, vmem),
        scratch_shapes=slots
        + [
            pltpu.VMEM((bits,) + small.shape, jnp.float32),
            pltpu.VMEM((bits + 1,) + small.shape, jnp.float32),
            pltpu.SemaphoreType.DMA((pieces, bits + 1)),
            pltpu.SemaphoreType.DMA((pieces, bits + 1)),
            pltpu.SemaphoreType.DMA((bits + 1,)),
            pltpu.SemaphoreType.DMA((bits + 1,)),
        ],
        compiler_params=pltpu.CompilerParams(
            collective_id=0, has_side_effects=True, vmem_limit_bytes=32 * 2**20
        ),
    )(*lefts, *rights, small)
    total = total.reshape(pieces, 2, block, width).transpose(2, 0, 1, 3).reshape(block, columns)
    return total, small_total


def local(
    tokens,
    cotangent,
    qkv_weight,
    qkv_moment,
    qkv_square,
    out_weight,
    out_moment,
    out_square,
    up_experts,
    up_moment,
    up_square,
    down_experts,
    down_moment,
    down_square,
    router_weight,
    router_moment,
    router_square,
    norm_gains,
    gain_moment,
    gain_square,
    relative_position_bias,
    bias_moment,
    bias_square,
    expert_ids,
    slot_ids,
):
    tok_rows, model_width = tokens.shape
    bucket_count, head_count = relative_position_bias.shape
    head_size = model_width // head_count
    score_scale = head_size ** (-0.5)
    expert_count = router_weight.shape[1]
    n_expert = lax.axis_size("expert")
    n_fsdp = lax.axis_size("fsdp")
    bits = n_expert.bit_length() - 1
    capacity = 2 * (5 * tok_rows // (4 * n_expert))
    seq_len = tok_rows * n_fsdp
    half = model_width // 2
    core = lax.axis_index("fsdp")
    own_index = lax.axis_index("expert") * n_fsdp + core
    qkv_other = swap(qkv_weight)
    out_other = swap(out_weight)
    inputs = tokens.astype(jnp.float32)
    upstream = cotangent.astype(jnp.float32)
    gain_one = norm_gains[0].astype(jnp.float32)
    gain_two = norm_gains[1].astype(jnp.float32)
    normed, inverse_one = norm_forward(inputs, gain_one)
    normed_low = normed.astype(jnp.bfloat16)

    def own_part(value):
        return lax.dynamic_slice_in_dim(value, core * half, half, 1)

    def other_part(value):
        return lax.dynamic_slice_in_dim(value, (1 - core) * half, half, 1)

    def times_halves(value, own, other):
        return jnp.dot(own_part(value), own, preferred_element_type=jnp.float32) + jnp.dot(
            other_part(value), other, preferred_element_type=jnp.float32
        )

    def times_transposed(value, own, other):
        first = jnp.where(core == 0, own, other)
        second = jnp.where(core == 0, other, own)
        return jnp.concatenate(
            [
                jnp.einsum("te,de->td", value, first, preferred_element_type=jnp.float32),
                jnp.einsum("te,de->td", value, second, preferred_element_type=jnp.float32),
            ],
            axis=1,
        )

    query_pos = core * tok_rows + jnp.arange(tok_rows, dtype=jnp.int32)
    other_pos = (1 - core) * tok_rows + jnp.arange(tok_rows, dtype=jnp.int32)
    key_pos = jnp.concatenate([query_pos, other_pos])
    bucket_range = jnp.arange(bucket_count, dtype=jnp.int32)
    indicator = (bucket_ids(query_pos, key_pos)[None] == bucket_range[:, None, None]).astype(
        jnp.bfloat16
    )
    bias_block = jnp.einsum(
        "yur,yv->vur", indicator, relative_position_bias, preferred_element_type=jnp.float32
    )
    qkv = times_halves(normed_low, qkv_weight, qkv_other).astype(jnp.bfloat16)
    key_value = qkv[:, model_width:]
    both = jnp.concatenate([key_value, swap(key_value)], axis=0)
    keys_heads = both[:, :model_width].reshape(seq_len, head_count, head_size)
    values_heads = both[:, model_width:].reshape(seq_len, head_count, head_size)
    queries = qkv[:, :model_width].reshape(tok_rows, head_count, head_size)
    scores = (
        jnp.einsum("qhd,khd->hqk", queries, keys_heads, preferred_element_type=jnp.float32)
        * score_scale
        + bias_block
    )
    log_total = jax.nn.logsumexp(scores, axis=-1, keepdims=True)
    prob_full = jnp.exp(scores - log_total)
    prob_low = prob_full.astype(jnp.bfloat16)
    context = (
        jnp.einsum("hqk,khd->qhd", prob_low, values_heads, preferred_element_type=jnp.float32)
        .astype(jnp.bfloat16)
        .reshape(tok_rows, model_width)
    )
    attention = times_halves(context, out_weight, out_other)
    middle = inputs + attention
    normed_two, inverse_two = norm_forward(middle, gain_two)
    router_float = router_weight.astype(jnp.float32)
    logits = jnp.dot(normed_two, router_float, precision=lax.Precision.HIGHEST)
    router_probs = jax.nn.softmax(logits, axis=-1)
    is_chosen = expert_ids[:, None] == jnp.arange(expert_count, dtype=jnp.int32)[None, :]
    gate_prob = jnp.sum(jnp.where(is_chosen, router_probs, 0.0), axis=1)
    slot_rows = n_expert * capacity
    row_range = jnp.arange(slot_rows, dtype=jnp.int32)
    row_expert = row_range // (2 * capacity)
    row_slot = row_range % capacity
    pick = (
        (row_expert[None, :] == expert_ids[:, None]) & (row_slot[None, :] == slot_ids[:, None])
    ).astype(jnp.bfloat16)
    token_rows = jnp.concatenate(
        [normed_two.astype(jnp.bfloat16), (gate_prob[:, None] * upstream).astype(jnp.bfloat16)],
        axis=1,
    )
    dispatched = jnp.einsum(
        "tr,td->rd", pick, token_rows, preferred_element_type=jnp.float32
    ).astype(jnp.bfloat16)
    arrived = lax.all_to_all(
        dispatched.reshape(n_expert, capacity, 2 * model_width),
        "expert",
        split_axis=0,
        concat_axis=0,
        tiled=True,
    ).reshape(slot_rows, 2 * model_width)
    up_local = up_experts[0]
    down_local = down_experts[0]
    gathered = jnp.concatenate([arrived, swap(arrived)], axis=0)
    expert_in = gathered[:, :model_width]
    grad_in = gathered[:, model_width:]
    pre_act = jnp.dot(expert_in, up_local, preferred_element_type=jnp.float32)
    activated = gelu_value(pre_act).astype(jnp.bfloat16)
    act_grad = jnp.einsum("rd,hd->rh", grad_in, down_local, preferred_element_type=jnp.float32)
    pre_grad = (act_grad * gelu_derivative(pre_act)).astype(jnp.bfloat16)
    partial_rows = jnp.concatenate(
        [
            jnp.dot(activated, down_local, preferred_element_type=jnp.float32),
            jnp.einsum("rh,dh->rd", pre_grad, up_local, preferred_element_type=jnp.float32),
        ],
        axis=1,
    )
    from_other = swap(partial_rows[slot_rows:].astype(jnp.bfloat16))
    summed = (partial_rows[:slot_rows] + from_other.astype(jnp.float32)).astype(jnp.bfloat16)
    returned = lax.all_to_all(
        summed.reshape(n_expert, capacity, 2 * model_width),
        "expert",
        split_axis=0,
        concat_axis=0,
        tiled=True,
    ).reshape(slot_rows, 2 * model_width)
    up_grad = jnp.einsum("rd,rh->dh", expert_in, pre_grad, preferred_element_type=jnp.float32)
    down_grad = jnp.einsum("rh,rd->hd", activated, grad_in, preferred_element_type=jnp.float32)
    mixed = jnp.dot(pick, returned, preferred_element_type=jnp.float32)
    picked = mixed[:, :model_width]
    dispatch_grad = mixed[:, model_width:]
    block_out = (middle + gate_prob[:, None] * picked).astype(jnp.bfloat16)
    gate_grad = jnp.sum(upstream * picked, axis=1)
    logit_grad = (gate_grad * gate_prob)[:, None] * (is_chosen.astype(jnp.float32) - router_probs)
    router_grad = jnp.dot(logit_grad.T, normed_two, precision=lax.Precision.HIGHEST)
    normed_two_grad = dispatch_grad + jnp.dot(
        logit_grad, router_float.T, precision=lax.Precision.HIGHEST
    )
    middle_part, gain_two_grad = norm_backward(middle, inverse_two, gain_two, normed_two_grad)
    middle_grad = upstream + middle_part
    attention_grad = middle_grad.astype(jnp.bfloat16)
    out_weight_grad = jnp.einsum(
        "td,te->de", context, attention_grad, preferred_element_type=jnp.float32
    )
    context_grad = (
        times_transposed(attention_grad, out_weight, out_other)
        .astype(jnp.bfloat16)
        .reshape(tok_rows, head_count, head_size)
    )
    prob_grad = jnp.einsum(
        "qhd,khd->hqk", context_grad, values_heads, preferred_element_type=jnp.float32
    )
    score_grad = (
        prob_full * (prob_grad - jnp.sum(prob_full * prob_grad, axis=-1, keepdims=True))
    ).astype(jnp.bfloat16)
    value_grad = jnp.einsum(
        "hqk,qhd->khd", prob_low, context_grad, preferred_element_type=jnp.float32
    ).reshape(seq_len, model_width)
    key_grad = (
        jnp.einsum("hqk,qhd->khd", score_grad, queries, preferred_element_type=jnp.float32)
        * score_scale
    ).reshape(seq_len, model_width)
    key_value_grad = jnp.concatenate([key_grad, value_grad], axis=1)
    key_value_own = (
        key_value_grad[:tok_rows]
        + swap(key_value_grad[tok_rows:].astype(jnp.bfloat16)).astype(jnp.float32)
    ).astype(jnp.bfloat16)
    query_grad = (
        (
            jnp.einsum("hqk,khd->qhd", score_grad, keys_heads, preferred_element_type=jnp.float32)
            * score_scale
        )
        .astype(jnp.bfloat16)
        .reshape(tok_rows, model_width)
    )
    table_grad = jnp.einsum(
        "evf,uvf->eu", indicator, score_grad, preferred_element_type=jnp.float32
    )
    qkv_grad = jnp.concatenate([query_grad, key_value_own], axis=1)

    def weight_grad(upstream_part):
        return jnp.einsum(
            "td,te->de", normed_low, upstream_part, preferred_element_type=jnp.float32
        )

    normed_grad = times_transposed(qkv_grad, qkv_weight, qkv_other)
    input_part, gain_one_grad = norm_backward(inputs, inverse_one, gain_one, normed_grad)
    tokens_grad = middle_grad + input_part
    table_size = bucket_count * head_count
    small = jnp.concatenate(
        [
            router_grad,
            gain_one_grad[None],
            gain_two_grad[None],
            jnp.pad(table_grad.reshape(1, table_size), ((0, 0), (0, model_width - table_size))),
        ],
        axis=0,
    )
    block = model_width // (n_expert * n_fsdp)
    if block % 8 == 0:
        small = jnp.pad(small, ((0, -small.shape[0] % 8), (0, 0)))
        weight_sum, small = owner_sum(
            (normed_low.T, context.T), (qkv_grad, attention_grad), small
        )
        qkv_sum = weight_sum[:, : 3 * model_width].reshape(1, -1)
        out_sum = weight_sum[:, 3 * model_width :].reshape(1, -1)
    else:
        upward = list(range(bits))
        small = sum_everywhere(small)
        qkv_sum = sum_to_owner(weight_grad(qkv_grad), upward).reshape(1, -1)
        out_sum = sum_to_owner(out_weight_grad, upward[1:] + upward[:1]).reshape(1, -1)
    router_sum = small[:expert_count].T
    gain_sum = small[expert_count : expert_count + 2]
    table_sum = small[expert_count + 2, :table_size].reshape(bucket_count, head_count)
    first_row = own_index * block
    owner_core = first_row // half
    local_row = first_row - owner_core * half

    def old_rows(own, other):
        own_rows = lax.dynamic_slice_in_dim(own, local_row, block, 0)
        other_rows = lax.dynamic_slice_in_dim(other, local_row, block, 0)
        rows = jnp.where(owner_core == core, own_rows, other_rows)
        return rows.astype(jnp.float32).reshape(1, -1)

    qkv_old = old_rows(qkv_weight, qkv_other)
    out_old = old_rows(out_weight, out_other)
    qkv_m, qkv_v, qkv_w = adam_step(
        qkv_old, qkv_moment, qkv_square, qkv_sum, 2.0 * model_width ** (-0.5), DECAY
    )
    out_m, out_v, out_w = adam_step(
        out_old, out_moment, out_square, out_sum, (seq_len / model_width) ** 0.5, DECAY
    )
    up_m, up_v, up_w = adam_step(
        up_experts.astype(jnp.float32),
        up_moment,
        up_square,
        up_grad[None],
        2.0 * model_width ** (-0.5),
        DECAY,
    )
    down_m, down_v, down_w = adam_step(
        down_experts.astype(jnp.float32),
        down_moment,
        down_square,
        down_grad[None],
        3.0 * expert_count * FF ** (-0.5),
        DECAY,
    )
    router_m, router_v, router_w = adam_step(
        router_float, router_moment, router_square, router_sum, model_width ** (-0.5), DECAY
    )
    gain_m, gain_v, gain_w = adam_step(
        norm_gains.astype(jnp.float32), gain_moment, gain_square, gain_sum, 0.5, 0.0
    )
    bias_m, bias_v, bias_w = adam_step(
        relative_position_bias.astype(jnp.float32), bias_moment, bias_square, table_sum, 2.0, 0.0
    )
    return (
        block_out,
        tokens_grad,
        qkv_m,
        qkv_v,
        qkv_w,
        out_m,
        out_v,
        out_w,
        up_m,
        up_v,
        up_w,
        down_m,
        down_v,
        down_w,
        router_m,
        router_v,
        router_w,
        gain_m,
        gain_v,
        gain_w,
        bias_m,
        bias_v,
        bias_w,
    )


def solution(mesh):
    return jax.shard_map(
        local,
        mesh=mesh,
        in_specs=(
            P(("expert", "fsdp"), None),
            P(("expert", "fsdp"), None),
            P("fsdp", None),
            P(("expert", "fsdp"), None),
            P(("expert", "fsdp"), None),
            P("fsdp", None),
            P(("expert", "fsdp"), None),
            P(("expert", "fsdp"), None),
            P("expert", None, "fsdp"),
            P("expert", None, "fsdp"),
            P("expert", None, "fsdp"),
            P("expert", "fsdp", None),
            P("expert", "fsdp", None),
            P("expert", "fsdp", None),
            P(),
            P(),
            P(),
            P(),
            P(),
            P(),
            P(),
            P(),
            P(),
            P(("expert", "fsdp")),
            P(("expert", "fsdp")),
        ),
        out_specs=(
            P(("expert", "fsdp"), None),
            P(("expert", "fsdp"), None),
            P(("expert", "fsdp"), None),
            P(("expert", "fsdp"), None),
            P(("expert", "fsdp"), None),
            P(("expert", "fsdp"), None),
            P(("expert", "fsdp"), None),
            P(("expert", "fsdp"), None),
            P("expert", None, "fsdp"),
            P("expert", None, "fsdp"),
            P("expert", None, "fsdp"),
            P("expert", "fsdp", None),
            P("expert", "fsdp", None),
            P("expert", "fsdp", None),
            P(),
            P(),
            P(),
            P(),
            P(),
            P(),
            P(),
            P(),
            P(),
        ),
        check_vma=False,
    )
```
